32 devices in a mesh: row: 4 (over y, core), col: 8 (over z, x).
Axes of the slice: x: 2, y: 2, z: 4, core: 2. Of those that a mesh axis runs over, the one named last changes fastest.
Arguments:
- queries: bfloat16 [4, 4096, 256], P(None, ('row', 'col'))
- probes: int32 [4, 4096, 2], P(None, ('row', 'col')), may hold values from 0 to 31, all different within a row; in each aligned block of 128 rows (0 to 127, 128 to 255, ..., all dimensions but the last counted through in order) at most 16 rows name the same one
- keys: bfloat16 [32, 1024, 256], P(('row', 'col')), may hold values from -6 to 6
- values: bfloat16 [32, 1024, 256], P(('row', 'col')), may hold values from -6 to 6
- bucket_home: int32 [32], replicated, may hold values from 0 to 31, each once
- bucket_rows: int32 [32], replicated, may hold values from 1 to 1024, 12288 in all
Outputs:
- attended: bfloat16 [4, 4096, 256], P(None, ('row', 'col'))
The draws below stay inside these ranges and needn't reach their ends.
Inputs may be any that keep to these rules, and one draw needn't show every extreme that they name: `probes`: each request names two different buckets; among the requests of one device in one step no bucket is named more than 16 times, a bound that some block reaches. `bucket_home`: each device holds exactly one bucket. `bucket_rows`: some bucket fills all 8 blocks.
All inputs are finite; a program needn't handle non-finite values.
Results may differ from the reference program's by a relative error of at most 0.007.
Values may be sent and summed in bfloat16 or wider, within the bound.
A program may use at most 64 MiB of HBM per device.

```python
import math
import jax
import jax.numpy as jnp
import numpy as np
from jax import lax

H = 8
HD = 32
D = 256
BLK = 128
SLOTS = 8
STEPS = 4
Q_DEV = 128
NB = 32
REQ = 4096
CAP = 16


def draw_queries(key, part):
    first_key = jax.random.fold_in(jax.random.fold_in(key, 11), 0)
    base = jax.random.normal(first_key, (STEPS, REQ, D), jnp.float32)
    return base.astype(jnp.bfloat16)


def level_of(own_key, extent, cuts, low, top_value):
    level, own = 1.0, jax.random.fold_in(own_key, 6)
    for dim, blocks in cuts:
        heights = jnp.exp(jax.random.uniform(jax.random.fold_in(own, dim), (blocks,), jnp.float32, low / len(cuts), top_value / len(cuts)))
        level = level * jnp.repeat(heights, extent[dim] // blocks).reshape([-1 if axis == dim else 1 for axis in range(len(extent))])
    return level


def split_up(count, total, bound, lean):
    portions = [(1 << 20) // math.isqrt(rank ** lean) + 1 for rank in range(2, count + 1)]
    surplus, holding = total - bound - (count - 1), [1] * (count - 1)
    while surplus > 0:
        free = [i for i in range(count - 1) if holding[i] < bound]
        mass, remaining = sum([portions[i] for i in free]), surplus
        for i in free:
            addition = min(bound - holding[i], max(1, remaining * portions[i] // mass), surplus)
            holding[i] = holding[i] + addition
            surplus = surplus - addition
    return np.array([bound] + holding)


def ragged_sizes(stream_key, amount, total, most, lean):
    if amount == 2:
        one = jax.random.randint(stream_key, (), max(1, total - most), min(most, total - 1) + 1)
        return jnp.stack([one, total - one])
    lengths = jnp.asarray(split_up(amount, total, most, lean), jnp.int32)
    couples = (amount - 1) // 2
    giver, sink = lengths[1:1 + 2 * couples:2], lengths[2:2 + 2 * couples:2]
    slack = jnp.minimum(giver - 1, most - sink)
    moved = jax.random.randint(jax.random.fold_in(stream_key, 1), (couples,), 0, 1 << 20) % (slack + 1)
    lengths = lengths.at[1:1 + 2 * couples:2].set(giver - moved).at[2:2 + 2 * couples:2].set(sink + moved)
    return lengths[jax.random.permutation(jax.random.fold_in(stream_key, 2), amount)]


def shared_out(own_key, own, number, rows, count, top, limit, lean):
    ranking = jax.random.permutation(own_key, count)
    crowded, usual = load_shares(count, rows * top, limit, lean, True), load_shares(count, rows * top, limit, lean, False)
    places = jnp.arange(count)

    def named(lengths, offset_by):
        used = int((lengths > 0).sum())
        fixed = max(1, used // 4)
        passed = fixed + (places - fixed + offset_by * (used - fixed)) % max(1, count - fixed)
        return jnp.zeros((count,), jnp.int32).at[ranking[jnp.where(places < fixed, places, passed)]].set(jnp.asarray(lengths, jnp.int32))

    lengths = jnp.where(number % 4 == 0, named(crowded, number // 4), named(usual, number - number // 4 - 1))
    mixed = jax.random.permutation(jax.random.fold_in(own, 3), count)
    source_of, receiver = mixed[0:count // 2 * 2:2], mixed[1:count // 2 * 2:2]
    margin = jnp.minimum(lengths[source_of] - 1, limit - lengths[receiver]) // 2
    margin = jnp.where((source_of == ranking[0]) | (receiver == ranking[0]) | (lengths[receiver] == 0), 0, jnp.maximum(margin, 0))
    passed = jax.random.randint(jax.random.fold_in(own, 4), (count // 2,), 0, 1 << 20) % (margin + 1)
    lengths = lengths.at[source_of].add(-passed).at[receiver].add(passed)
    labels = jnp.searchsorted(jnp.cumsum(lengths), jnp.arange(rows * top), side="right").astype(jnp.int32)
    table = labels.reshape(top, rows).T
    table = table[jax.random.permutation(jax.random.fold_in(own, 1), rows)]
    offset_by = jax.random.randint(jax.random.fold_in(own, 2), (rows, 1), 0, top)
    return jnp.take_along_axis(table, (jnp.arange(top)[None, :] + offset_by) % top, axis=1)


def load_shares(amount, total, most, slope, full):
    portions = [(1 << 20) // math.isqrt(rank ** slope) + 1 for rank in range(1, amount + 1)]
    largest = most if full else min(most, max(-(-total // amount), total * portions[0] // sum(portions)))
    least = 1 if total - largest >= amount - 1 else 0
    holding, spare = [largest] + [least] * (amount - 1), total - largest - least * (amount - 1)
    while spare > 0:
        movable = [i for i in range(1, amount) if holding[i] < largest] or [i for i in range(1, amount) if holding[i] < most]
        whole, left = sum([portions[i] for i in movable]), spare
        for i in movable:
            extra = min(most - holding[i], max(1, left * portions[i] // whole), spare)
            holding[i] = holding[i] + extra
            spare = spare - extra
    return np.array(holding)


def gaussian(key, dims, scale, most, shards=(), kind=jnp.bfloat16):
    result = scale * jax.random.normal(key, dims, jnp.float32)
    if shards:
        result = result * level_of(key, dims, shards, -0.22, 0.18)
    return jnp.clip(result, -most, most).astype(kind)


def setup_inputs(seed: int = 0) -> dict:
    seeds = jax.random.split(jax.random.key(seed), 7)
    queries = draw_queries(jax.random.fold_in(seeds[6], 71), 0)
    probes_keys = jax.random.split(jax.random.fold_in(seeds[1], 1), STEPS * REQ // Q_DEV)
    probes_turns = jax.random.permutation(jax.random.fold_in(seeds[1], 3), STEPS * REQ // Q_DEV)
    probes = jax.vmap(lambda own, number: shared_out(jax.random.fold_in(seeds[1], 2), own, number, Q_DEV, NB, 2, CAP, 2))(probes_keys, probes_turns).reshape((STEPS, REQ, 2))
    keys = gaussian(seeds[2], (NB, SLOTS * BLK, D), 1.0, 6.0, ((0, 32),))
    values = gaussian(seeds[3], (NB, SLOTS * BLK, D), 1.0, 6.0, ((0, 32),))
    bucket_home = jax.random.permutation(seeds[4], NB).astype(jnp.int32)
    bucket_rows = ragged_sizes(seeds[5], NB, NB * SLOTS * BLK * 3 // 8, SLOTS * BLK, 2).astype(jnp.int32)
    return {"queries": queries, "probes": probes, "keys": keys, "values": values, "bucket_home": bucket_home, "bucket_rows": bucket_rows}


def reference(queries, probes, keys, values, bucket_home, bucket_rows):
    score_scale = 1.0 / math.sqrt(HD)
    total_rows = SLOTS * BLK
    group_size = math.gcd(STEPS * REQ, 64)
    groups = STEPS * REQ // group_size
    query_groups = queries.reshape(groups, group_size, D)
    probe_groups = probes.reshape(groups, group_size, 2)

    def one_group(pieces):
        query_block, probe_block = pieces
        device_ids = bucket_home[probe_block]
        key_rows = keys[device_ids].astype(jnp.float32).reshape(group_size, 2 * total_rows, H, HD)
        value_rows = values[device_ids].astype(jnp.float32).reshape(group_size, 2 * total_rows, H, HD)
        limits = bucket_rows[probe_block]
        valid_rows = (jnp.arange(total_rows, dtype=jnp.int32)[None, None, :] < limits[:, :, None]).reshape(group_size, 2 * total_rows)
        query_heads = query_block.astype(jnp.float32).reshape(group_size, H, HD)
        scores = jnp.einsum('bhd,bkhd->bhk', query_heads, key_rows) * score_scale
        scores = jnp.where(valid_rows[:, None, :], scores, -jnp.inf)
        highest = lax.optimization_barrier(jnp.max(scores, axis=-1, keepdims=True))
        weights = jnp.exp(scores - highest)
        total = lax.optimization_barrier(jnp.sum(weights, axis=-1))
        rounded = lax.optimization_barrier(weights.astype(jnp.bfloat16)).astype(jnp.float32)
        mixed = jnp.einsum('bhk,bkhd->bhd', rounded, value_rows) / total[:, :, None]
        return mixed.reshape(group_size, D).astype(jnp.bfloat16)
    attended = lax.map(one_group, (query_groups, probe_groups))
    return attended.reshape(STEPS, REQ, D)
```

```python
import functools
import math

import jax
import jax.numpy as jnp
from jax import lax
from jax.experimental import pallas as pl
from jax.experimental.pallas import tpu as pltpu
from jax.sharding import PartitionSpec as P

HD = 32
LANES = 128
ROWS = 16
TILE = 256
MESH = pl.DeviceIdType.MESH
bf16 = jnp.bfloat16
f32 = jnp.float32


def iota(shape, dim):
    return lax.broadcasted_iota(jnp.int32, shape, dim)


def kernel(
    dims, q_ref, probe_ref, home_ref, rows_ref, k_ref, v_ref, out_ref,
    keys_by_head, values_by_head, pos_ref, send, recv, back, answer, mass_back, mass_answer,
    send_sem, recv_sem, back_sem, answer_sem, mass_back_sem, mass_answer_sem,
):
    n, ncol, steps, nq, width, cap, per_phase, phases = dims
    heads = width // HD
    key_rows = k_ref.shape[0]
    slots = n * ROWS
    scale = math.log2(math.e) / math.sqrt(HD)
    me = lax.axis_index("row") * ncol + lax.axis_index("col")

    def peer(index):
        other = lax.rem(me + index, n)
        return other, (other // ncol, lax.rem(other, ncol))

    barrier = pltpu.get_barrier_semaphore()

    @pl.loop(1, n)
    def _(index):
        _, where = peer(index)
        pl.semaphore_signal(barrier, inc=1, device_id=where, device_id_type=MESH)

    def copy_to(index, phase, source, target, source_sem, target_sem):
        other, where = peer(index)
        return pltpu.make_async_remote_copy(
            src_ref=source.at[phase, other],
            dst_ref=target.at[phase, me],
            send_sem=source_sem.at[phase],
            recv_sem=target_sem.at[phase],
            device_id=where,
            device_id_type=MESH,
        )

    def all_copies(phase, source, target, source_sem, target_sem):
        _, where = peer(1)
        return pltpu.make_async_remote_copy(
            src_ref=source.at[phase, pl.ds(0, n - 1)],
            dst_ref=target.at[phase, pl.ds(0, n - 1)],
            send_sem=source_sem.at[phase],
            recv_sem=target_sem.at[phase],
            device_id=where,
            device_id_type=MESH,
        )

    queries_out = (send, recv, send_sem, recv_sem)
    answers_out = (back, answer, back_sem, answer_sem)
    masses_out = (mass_back, mass_answer, mass_back_sem, mass_answer_sem)

    home_row = home_ref[...]
    diagonal = iota((n, n), 0) == iota((n, n), 1)
    home_column = jnp.sum(jnp.where(diagonal, home_row, 0), axis=1, keepdims=True).astype(f32)
    before = (iota((nq, nq), 0) < iota((nq, nq), 1)).astype(bf16)

    def slot_rows(step):
        ids = probe_ref[step]
        first = (iota((n, nq), 0) == ids[0:1, :]).astype(f32)
        second = (iota((n, nq), 0) == ids[1:2, :]).astype(f32)
        both = jnp.concatenate([first, second], axis=0).astype(bf16)
        earlier = jnp.dot(both, before, preferred_element_type=f32)
        offset = jnp.sum(first, axis=1, keepdims=True)
        order_first = jnp.sum(first * (earlier[:n] + home_column * ROWS), axis=0, keepdims=True)
        order_second = jnp.sum(
            second * (earlier[n:] + offset + home_column * ROWS), axis=0, keepdims=True
        )
        shift = (step % per_phase) * cap
        return jnp.concatenate([order_first, order_second], axis=0).astype(jnp.int32) + shift

    def arrange(phase):
        total = None
        for local in range(per_phase):
            step = phase * per_phase + local
            pos = slot_rows(step)
            pos_ref[step] = pos
            places = iota((slots, nq), 0)
            match = ((places == pos[0:1, :]) | (places == pos[1:2, :])).astype(f32).astype(bf16)
            part = jnp.dot(match, q_ref[step], preferred_element_type=f32)
            total = part if total is None else total + part
        send[phase] = total.astype(bf16).reshape(n, ROWS, width)

    for phase in range(phases):
        arrange(phase)
        if phase == 0:
            pl.semaphore_wait(barrier, n - 1)

        @pl.loop(1, n)
        def _(index):
            copy_to(index, phase, *queries_out).start()

    mine = jnp.sum(jnp.where(home_row == me, rows_ref[...], 0), axis=1, keepdims=True)
    valid = iota((key_rows, width), 0) < mine
    keys_all = k_ref[...].astype(f32)
    keys_all = jnp.where(valid, keys_all, keys_all[0:1, :]).T
    values_all = jnp.where(valid, v_ref[...].astype(f32), 0.0)
    counted = jnp.where(valid, 1.0, 0.0)
    for head in range(heads):
        keys_by_head[head] = jnp.where(
            iota((width, key_rows), 0) // HD == head, keys_all, 0.0
        ).astype(bf16)
        values_by_head[head] = jnp.where(
            iota((key_rows, width), 1) // HD == head, values_all, counted
        ).astype(bf16)

    lane = iota((TILE, LANES), 1)
    group = LANES // HD

    def attend(phase, tile):
        devices = TILE // ROWS
        start = pl.multiple_of(tile * devices, devices)
        queries = recv[phase, pl.ds(start, devices)].reshape(TILE, width)
        halves = [jnp.zeros((TILE, LANES), f32) for _ in range(width // LANES)]
        masses = jnp.ones((TILE, LANES), f32)
        tops = jnp.zeros((TILE, LANES), f32)
        for head in range(heads):
            scores = jnp.dot(queries, keys_by_head[head], preferred_element_type=f32)
            top = jnp.max(scores, axis=1, keepdims=True)
            weights = jnp.exp2((scores - top) * scale).astype(bf16)
            mixed = jnp.dot(weights, values_by_head[head], preferred_element_type=f32)
            at = head // group
            other = (at + 1) % (width // LANES)
            total = mixed[:, other * LANES:(other + 1) * LANES]
            piece = mixed[:, at * LANES:(at + 1) * LANES]
            halves[at] = jnp.where(lane // HD == head % group, piece / total, halves[at])
            masses = jnp.where(lane // ROWS == head, total, masses)
            tops = jnp.where(lane // ROWS == head, top, tops)
        back[phase, pl.ds(start, devices)] = (
            jnp.concatenate(halves, axis=1).astype(bf16).reshape(devices, ROWS, width)
        )
        logs = tops * scale + jnp.log2(masses)
        logs = jnp.where(lane % ROWS == iota((TILE, LANES), 0) % ROWS, logs, 0.0)
        mass_back[phase, pl.ds(start, devices)] = jnp.sum(
            logs.reshape(devices, ROWS, LANES), axis=1, keepdims=True
        )

    @pl.loop(0, phases)
    def _(phase):
        all_copies(phase, *queries_out).wait_recv()
        recv[phase, me] = send[phase, me]

        @pl.loop(0, slots // TILE)
        def _(tile):
            attend(phase, tile)

        @pl.loop(1, n)
        def _(index):
            copy_to(index, phase, *answers_out).start()
            copy_to(index, phase, *masses_out).start()

    spread = (iota((LANES, width), 0) // ROWS == iota((LANES, width), 1) // HD).astype(f32).astype(bf16)
    own_lane = iota((n, ROWS, LANES), 2) % ROWS == iota((n, ROWS, LANES), 1)

    @pl.loop(0, phases)
    def _(phase):
        all_copies(phase, *answers_out).wait_recv()
        all_copies(phase, *masses_out).wait_recv()
        answer[phase, me] = back[phase, me]
        mass_answer[phase, me] = mass_back[phase, me]
        outs = answer[phase].reshape(slots, width)
        rest = jnp.where(own_lane, mass_answer[phase], 0.0).reshape(slots, LANES)
        columns = [outs]
        for _ in range(3):
            part = rest.astype(bf16)
            columns.append(part)
            rest = rest - part.astype(f32)
        for local in range(per_phase):
            step = phase * per_phase + local
            pos = pos_ref[step]
            places = iota((slots, nq), 0)
            match = jnp.concatenate(
                [(places == pos[0:1, :]).astype(f32), (places == pos[1:2, :]).astype(f32)], axis=1
            ).astype(bf16)
            picked = [
                lax.dot_general(match, c, (((0,), (0,)), ((), ())), preferred_element_type=f32)
                for c in columns
            ]
            logs = sum(
                jnp.dot(part.astype(bf16), spread, preferred_element_type=f32)
                for part in picked[1:]
            )
            share = 1.0 / (1.0 + jnp.exp2(logs[nq:] - logs[:nq]))
            merged = picked[0][nq:] + share * (picked[0][:nq] - picked[0][nq:])
            out_ref[step] = merged.astype(bf16)

    @pl.loop(0, phases)
    def _(phase):
        all_copies(phase, *queries_out).wait_send()
        all_copies(phase, *answers_out).wait_send()
        all_copies(phase, *masses_out).wait_send()


def body(ncol, n, queries, probes, keys, values, bucket_home, bucket_rows):
    steps, nq, width = queries.shape
    cap = max(1, 4 * nq // n)
    per_phase = min(steps, max(1, ROWS // cap))
    phases = steps // per_phase
    key_rows = keys.shape[1]
    heads = width // HD
    dims = (n, ncol, steps, nq, width, cap, per_phase, phases)
    vmem = pl.BlockSpec(memory_space=pltpu.VMEM)
    block = pltpu.VMEM((phases, n, ROWS, width), bf16)
    mass = pltpu.VMEM((phases, n, 1, LANES), f32)
    slots = phases * n * ROWS
    return pl.pallas_call(
        functools.partial(kernel, dims),
        out_shape=jax.ShapeDtypeStruct((steps, nq, width), bf16),
        in_specs=[vmem] * 6,
        out_specs=vmem,
        scratch_shapes=[
            pltpu.VMEM((heads, width, key_rows), bf16),
            pltpu.VMEM((heads, key_rows, width), bf16),
            pltpu.VMEM((steps, 2, nq), jnp.int32),
            block, block, block, block, mass, mass,
        ] + [pltpu.SemaphoreType.DMA((phases,))] * 6,
        compiler_params=pltpu.CompilerParams(
            collective_id=0, has_side_effects=True, vmem_limit_bytes=56 * 1024 * 1024
        ),
        cost_estimate=pl.CostEstimate(
            flops=4 * slots * key_rows * width * heads,
            bytes_accessed=4 * key_rows * width,
            transcendentals=slots * key_rows * heads,
        ),
    )(
        queries,
        jnp.transpose(probes, (0, 2, 1)),
        bucket_home.reshape(1, n),
        bucket_rows.reshape(1, n),
        keys[0],
        values[0],
    )


def solution(mesh):
    ncol = mesh.shape["col"]
    n = mesh.shape["row"] * ncol
    return jax.shard_map(
        functools.partial(body, ncol, n),
        mesh=mesh,
        in_specs=(
            P(None, ("row", "col"), None),
            P(None, ("row", "col"), None),
            P(("row", "col"), None, None),
            P(("row", "col"), None, None),
            P(),
            P(),
        ),
        out_specs=P(None, ("row", "col"), None),
        check_vma=False,
    )
```

```python
import functools
import math

import jax
import jax.numpy as jnp
from jax import lax
from jax.experimental import pallas as pl
from jax.experimental.pallas import tpu as pltpu
from jax.sharding import PartitionSpec as P

HD = 32
LANES = 128
ROWS = 16
TILE = 256
MESH = pl.DeviceIdType.MESH
bf16 = jnp.bfloat16
f32 = jnp.float32


def iota(shape, dim):
    return lax.broadcasted_iota(jnp.int32, shape, dim)


def kernel(
    dims, q_ref, probe_ref, home_ref, rows_ref, k_ref, v_ref, out_ref,
    keys_by_head, values_by_head, pos_ref, send, recv, back, answer, mass_back, mass_answer,
    send_sem, recv_sem, back_sem, answer_sem, mass_back_sem, mass_answer_sem,
):
    n, ncol, steps, nq, width, cap, per_phase, phases = dims
    heads = width // HD
    key_rows = k_ref.shape[0]
    slots = n * ROWS
    scale = math.log2(math.e) / math.sqrt(HD)
    me = lax.axis_index("row") * ncol + lax.axis_index("col")

    def peer(index):
        other = lax.rem(me + index, n)
        return other, (other // ncol, lax.rem(other, ncol))

    barrier = pltpu.get_barrier_semaphore()

    @pl.loop(1, n)
    def _(index):
        _, where = peer(index)
        pl.semaphore_signal(barrier, inc=1, device_id=where, device_id_type=MESH)

    def copy_to(index, phase, source, target, source_sem, target_sem):
        other, where = peer(index)
        return pltpu.make_async_remote_copy(
            src_ref=source.at[phase, other],
            dst_ref=target.at[phase, me],
            send_sem=source_sem.at[phase],
            recv_sem=target_sem.at[phase],
            device_id=where,
            device_id_type=MESH,
        )

    def all_copies(phase, source, target, source_sem, target_sem):
        _, where = peer(1)
        return pltpu.make_async_remote_copy(
            src_ref=source.at[phase, pl.ds(0, n - 1)],
            dst_ref=target.at[phase, pl.ds(0, n - 1)],
            send_sem=source_sem.at[phase],
            recv_sem=target_sem.at[phase],
            device_id=where,
            device_id_type=MESH,
        )

    queries_out = (send, recv, send_sem, recv_sem)
    answers_out = (back, answer, back_sem, answer_sem)
    masses_out = (mass_back, mass_answer, mass_back_sem, mass_answer_sem)

    home_row = home_ref[...]
    diagonal = iota((n, n), 0) == iota((n, n), 1)
    home_column = jnp.sum(jnp.where(diagonal, home_row, 0), axis=1, keepdims=True).astype(f32)
    before = (iota((nq, nq), 0) < iota((nq, nq), 1)).astype(bf16)

    def slot_rows(step):
        ids = probe_ref[step]
        first = (iota((n, nq), 0) == ids[0:1, :]).astype(f32)
        second = (iota((n, nq), 0) == ids[1:2, :]).astype(f32)
        both = jnp.concatenate([first, second], axis=0).astype(bf16)
        earlier = jnp.dot(both, before, preferred_element_type=f32)
        offset = jnp.sum(first, axis=1, keepdims=True)
        order_first = jnp.sum(first * (earlier[:n] + home_column * ROWS), axis=0, keepdims=True)
        order_second = jnp.sum(
            second * (earlier[n:] + offset + home_column * ROWS), axis=0, keepdims=True
        )
        shift = (step % per_phase) * cap
        return jnp.concatenate([order_first, order_second], axis=0).astype(jnp.int32) + shift

    def arrange(phase):
        total = None
        for local in range(per_phase):
            step = phase * per_phase + local
            pos = slot_rows(step)
            pos_ref[step] = pos
            places = iota((slots, nq), 0)
            match = ((places == pos[0:1, :]) | (places == pos[1:2, :])).astype(f32).astype(bf16)
            part = jnp.dot(match, q_ref[step], preferred_element_type=f32)
            total = part if total is None else total + part
        send[phase] = total.astype(bf16).reshape(n, ROWS, width)

    def send_queries(phase):
        @pl.loop(1, n)
        def _(index):
            copy_to(index, phase, *queries_out).start()

    arrange(0)
    pl.semaphore_wait(barrier, n - 1)
    send_queries(0)

    @pl.loop(1, phases)
    def _(phase):
        arrange(phase)
        send_queries(phase)

    mine = jnp.sum(jnp.where(home_row == me, rows_ref[...], 0), axis=1, keepdims=True)
    valid = iota((key_rows, width), 0) < mine
    keys_all = k_ref[...].astype(f32)
    keys_all = jnp.where(valid, keys_all, keys_all[0:1, :])
    values_all = jnp.where(valid, v_ref[...].astype(f32), 0.0).T
    counted = (iota((ROWS, key_rows), 1) < mine).astype(f32)
    for head in range(heads):
        keys_by_head[head] = jnp.where(
            iota((key_rows, width), 1) // HD == head, keys_all, 0.0
        ).astype(bf16)
        values_by_head[head] = jnp.concatenate(
            [values_all[head * HD:(head + 1) * HD], counted], axis=0
        ).astype(bf16)

    def attend(phase, tile):
        devices = TILE // ROWS
        start = pl.multiple_of(tile * devices, devices)
        queries = recv[phase, pl.ds(start, devices)].reshape(TILE, width)
        queries = queries.astype(f32).T.astype(bf16)
        pieces, logs = [], []
        following = jnp.dot(keys_by_head[0], queries, preferred_element_type=f32)
        for head in range(heads):
            scores = following
            if head + 1 < heads:
                following = jnp.dot(keys_by_head[head + 1], queries, preferred_element_type=f32)
            top = jnp.max(scores, axis=0, keepdims=True)
            weights = jnp.exp2((scores - top) * scale).astype(bf16)
            mixed = jnp.dot(values_by_head[head], weights, preferred_element_type=f32)
            total = mixed[HD:HD + 1]
            pieces.append(mixed[:HD] * (1.0 / total))
            logs.append(jnp.broadcast_to(top * scale + jnp.log2(total), (ROWS, TILE)))
        back[phase, pl.ds(start, devices)] = (
            jnp.concatenate(pieces, axis=0).T.astype(bf16).reshape(devices, ROWS, width)
        )
        logs = jnp.concatenate(logs, axis=0).T
        logs = jnp.where(
            iota((TILE, LANES), 1) % ROWS == iota((TILE, LANES), 0) % ROWS, logs, 0.0
        )
        mass_back[phase, pl.ds(start, devices)] = jnp.sum(
            logs.reshape(devices, ROWS, LANES), axis=1, keepdims=True
        )

    @pl.loop(0, phases)
    def _(phase):
        all_copies(phase, *queries_out).wait_recv()
        recv[phase, me] = send[phase, me]

        @pl.loop(0, slots // TILE)
        def _(tile):
            attend(phase, tile)

        @pl.loop(1, n)
        def _(index):
            copy_to(index, phase, *answers_out).start()
            copy_to(index, phase, *masses_out).start()

    spread = (iota((LANES, width), 0) // ROWS == iota((LANES, width), 1) // HD).astype(f32).astype(bf16)
    own_lane = iota((n, ROWS, LANES), 2) % ROWS == iota((n, ROWS, LANES), 1)

    @pl.loop(0, phases)
    def _(phase):
        all_copies(phase, *answers_out).wait_recv()
        all_copies(phase, *masses_out).wait_recv()
        answer[phase, me] = back[phase, me]
        mass_answer[phase, me] = mass_back[phase, me]
        outs = answer[phase].reshape(slots, width)
        rest = jnp.where(own_lane, mass_answer[phase], 0.0).reshape(slots, LANES)
        columns = [outs]
        for _ in range(3):
            part = rest.astype(bf16)
            columns.append(part)
            rest = rest - part.astype(f32)
        for local in range(per_phase):
            step = phase * per_phase + local
            pos = pos_ref[step]
            places = iota((slots, nq), 0)
            match = jnp.concatenate(
                [(places == pos[0:1, :]).astype(f32), (places == pos[1:2, :]).astype(f32)], axis=1
            ).astype(bf16)
            picked = [
                lax.dot_general(match, c, (((0,), (0,)), ((), ())), preferred_element_type=f32)
                for c in columns
            ]
            logs = sum(
                jnp.dot(part.astype(bf16), spread, preferred_element_type=f32)
                for part in picked[1:]
            )
            share = 1.0 / (1.0 + jnp.exp2(logs[nq:] - logs[:nq]))
            merged = picked[0][nq:] + share * (picked[0][:nq] - picked[0][nq:])
            out_ref[step] = merged.astype(bf16)

    @pl.loop(0, phases)
    def _(phase):
        all_copies(phase, *queries_out).wait_send()
        all_copies(phase, *answers_out).wait_send()
        all_copies(phase, *masses_out).wait_send()


def body(ncol, n, queries, probes, keys, values, bucket_home, bucket_rows):
    steps, nq, width = queries.shape
    cap = max(1, 4 * nq // n)
    per_phase = min(steps, max(1, ROWS // cap))
    phases = steps // per_phase
    key_rows = keys.shape[1]
    heads = width // HD
    dims = (n, ncol, steps, nq, width, cap, per_phase, phases)
    vmem = pl.BlockSpec(memory_space=pltpu.VMEM)
    block = pltpu.VMEM((phases, n, ROWS, width), bf16)
    mass = pltpu.VMEM((phases, n, 1, LANES), f32)
    slots = phases * n * ROWS
    return pl.pallas_call(
        functools.partial(kernel, dims),
        out_shape=jax.ShapeDtypeStruct((steps, nq, width), bf16),
        in_specs=[vmem] * 6,
        out_specs=vmem,
        scratch_shapes=[
            pltpu.VMEM((heads, key_rows, width), bf16),
            pltpu.VMEM((heads, HD + ROWS, key_rows), bf16),
            pltpu.VMEM((steps, 2, nq), jnp.int32),
            block, block, block, block, mass, mass,
        ] + [pltpu.SemaphoreType.DMA((phases,))] * 6,
        compiler_params=pltpu.CompilerParams(
            collective_id=0, has_side_effects=True, vmem_limit_bytes=56 * 1024 * 1024
        ),
        cost_estimate=pl.CostEstimate(
            flops=4 * slots * key_rows * width * heads,
            bytes_accessed=4 * key_rows * width,
            transcendentals=slots * key_rows * heads,
        ),
    )(
        queries,
        jnp.transpose(probes, (0, 2, 1)),
        bucket_home.reshape(1, n),
        bucket_rows.reshape(1, n),
        keys[0],
        values[0],
    )


def solution(mesh):
    ncol = mesh.shape["col"]
    n = mesh.shape["row"] * ncol
    return jax.shard_map(
        functools.partial(body, ncol, n),
        mesh=mesh,
        in_specs=(
            P(None, ("row", "col"), None),
            P(None, ("row", "col"), None),
            P(("row", "col"), None, None),
            P(("row", "col"), None, None),
            P(),
            P(),
        ),
        out_specs=P(None, ("row", "col"), None),
        check_vma=False,
    )
```

```python
import functools
import math

import jax
import jax.numpy as jnp
from jax import lax
from jax.experimental import pallas as pl
from jax.experimental.pallas import tpu as pltpu
from jax.sharding import PartitionSpec as P

HD = 32
LANES = 128
ROWS = 16
TILE = 256
MESH = pl.DeviceIdType.MESH
bf16 = jnp.bfloat16
f32 = jnp.float32


def iota(shape, dim):
    return lax.broadcasted_iota(jnp.int32, shape, dim)


def kernel(
    dims, q_ref, probe_ref, home_ref, rows_ref, k_ref, v_ref, out_ref,
    keys_by_head, values_by_head, pos_ref, far_q, far_probe,
    send, recv, back, answer, mass_back, mass_answer, half_out, far_out, half_mass, far_mass,
    send_sem, recv_sem, back_sem, answer_sem, mass_back_sem, mass_answer_sem,
    q_sem, far_q_sem, half_sem, far_sem, half_mass_sem, far_mass_sem, probe_sem, far_probe_sem,
):
    n, ncol, steps, nq, width, cap, per_phase, phases = dims
    heads = width // HD
    key_rows = k_ref.shape[0]
    hcol = ncol // 2
    m = n // 2
    slots = m * ROWS
    scale = math.log2(math.e) / math.sqrt(HD)
    row, col = lax.axis_index("row"), lax.axis_index("col")
    device = row * ncol + col
    half = col // hcol
    me = row * hcol + lax.rem(col, hcol)
    mirror = (row, lax.rem(col + hcol, ncol))

    def peer(index):
        other = lax.rem(me + index, m)
        return other, (other // hcol, half * hcol + lax.rem(other, hcol))

    barrier = pltpu.get_barrier_semaphore()
    pl.semaphore_signal(barrier, inc=1, device_id=mirror, device_id_type=MESH)

    @pl.loop(1, m)
    def _(index):
        _, where = peer(index)
        pl.semaphore_signal(barrier, inc=1, device_id=where, device_id_type=MESH)

    def copy_to(index, unit, source, target, source_sem, target_sem):
        other, where = peer(index)
        return pltpu.make_async_remote_copy(
            src_ref=source.at[unit, other],
            dst_ref=target.at[unit, me],
            send_sem=source_sem.at[unit],
            recv_sem=target_sem.at[unit],
            device_id=where,
            device_id_type=MESH,
        )

    def all_copies(unit, source, target, source_sem, target_sem):
        _, where = peer(1)
        return pltpu.make_async_remote_copy(
            src_ref=source.at[unit, pl.ds(0, m - 1)],
            dst_ref=target.at[unit, pl.ds(0, m - 1)],
            send_sem=source_sem.at[unit],
            recv_sem=target_sem.at[unit],
            device_id=where,
            device_id_type=MESH,
        )

    def mirrored(phase, source, target, source_sem, target_sem):
        part = pl.ds(phase * per_phase, per_phase)
        return pltpu.make_async_remote_copy(
            src_ref=source.at[part],
            dst_ref=target.at[part],
            send_sem=source_sem.at[phase],
            recv_sem=target_sem.at[phase],
            device_id=mirror,
            device_id_type=MESH,
        )

    queries_out = (send, recv, send_sem, recv_sem)
    answers_out = (back, answer, back_sem, answer_sem)
    masses_out = (mass_back, mass_answer, mass_back_sem, mass_answer_sem)
    far_queries = (q_ref, far_q, q_sem, far_q_sem)
    far_answers = (half_out, far_out, half_sem, far_sem)
    far_masses = (half_mass, far_mass, half_mass_sem, far_mass_sem)
    far_probes = pltpu.make_async_remote_copy(
        src_ref=probe_ref, dst_ref=far_probe, send_sem=probe_sem.at[0], recv_sem=far_probe_sem.at[0],
        device_id=mirror, device_id_type=MESH,
    )

    home_row = home_ref[...]
    home_col = home_row % ncol
    base_row = jnp.where(
        home_col // hcol == half, (home_row // ncol * hcol + home_col % hcol) * ROWS, -(1 << 20)
    )
    diagonal = iota((n, n), 0) == iota((n, n), 1)
    base = jnp.sum(jnp.where(diagonal, base_row, 0), axis=1, keepdims=True).astype(f32)
    before = (iota((nq, nq), 0) < iota((nq, nq), 1)).astype(bf16)

    def slot_rows(ids, local):
        first = (iota((n, nq), 0) == ids[0:1, :]).astype(f32)
        second = (iota((n, nq), 0) == ids[1:2, :]).astype(f32)
        both = jnp.concatenate([first, second], axis=0).astype(bf16)
        earlier = jnp.dot(both, before, preferred_element_type=f32)
        offset = jnp.sum(first, axis=1, keepdims=True)
        order_first = jnp.sum(first * (earlier[:n] + base), axis=0, keepdims=True)
        order_second = jnp.sum(second * (earlier[n:] + offset + base), axis=0, keepdims=True)
        return jnp.concatenate([order_first, order_second], axis=0).astype(jnp.int32) + local * cap

    def send_queries(group, phase):
        total = None
        for local in range(per_phase):
            step = phase * per_phase + local
            pos = slot_rows((far_probe if group else probe_ref)[step], local)
            pos_ref[group, step] = pos
            places = iota((slots, nq), 0)
            match = ((places == pos[0:1, :]) | (places == pos[1:2, :])).astype(f32).astype(bf16)
            part = jnp.dot(match, (far_q if group else q_ref)[step], preferred_element_type=f32)
            total = part if total is None else total + part
        send[2 * phase + group] = total.astype(bf16).reshape(m, ROWS, width)

        @pl.loop(1, m)
        def _(index):
            copy_to(index, 2 * phase + group, *queries_out).start()

    pl.semaphore_wait(barrier, m)
    far_probes.start()
    for phase in range(phases):
        mirrored(phase, *far_queries).start()

    @pl.loop(0, phases)
    def _(phase):
        send_queries(0, phase)

    mine = jnp.sum(jnp.where(home_row == device, rows_ref[...], 0), axis=1, keepdims=True)
    valid = iota((key_rows, width), 0) < mine
    keys_all = k_ref[...].astype(f32)
    keys_all = jnp.where(valid, keys_all, keys_all[0:1, :])
    values_all = jnp.where(valid, v_ref[...].astype(f32), 0.0).T
    counted = (iota((ROWS, key_rows), 1) < mine).astype(f32)
    for head in range(heads):
        keys_by_head[head] = jnp.where(
            iota((key_rows, width), 1) // HD == head, keys_all, 0.0
        ).astype(bf16)
        values_by_head[head] = jnp.concatenate(
            [values_all[head * HD:(head + 1) * HD], counted], axis=0
        ).astype(bf16)

    def attend(unit, tile):
        devices = TILE // ROWS
        start = pl.multiple_of(tile * devices, devices)
        queries = recv[unit, pl.ds(start, devices)].reshape(TILE, width)
        queries = queries.astype(f32).T.astype(bf16)
        pieces, logs = [], []
        following = jnp.dot(keys_by_head[0], queries, preferred_element_type=f32)
        for head in range(heads):
            scores = following
            if head + 1 < heads:
                following = jnp.dot(keys_by_head[head + 1], queries, preferred_element_type=f32)
            top = jnp.max(scores, axis=0, keepdims=True)
            weights = jnp.exp2((scores - top) * scale).astype(bf16)
            mixed = jnp.dot(values_by_head[head], weights, preferred_element_type=f32)
            total = mixed[HD:HD + 1]
            pieces.append(mixed[:HD] * (1.0 / total))
            logs.append(jnp.broadcast_to(top * scale + jnp.log2(total), (ROWS, TILE)))
        back[unit, pl.ds(start, devices)] = (
            jnp.concatenate(pieces, axis=0).T.astype(bf16).reshape(devices, ROWS, width)
        )
        logs = jnp.concatenate(logs, axis=0).T
        logs = jnp.where(
            iota((TILE, LANES), 1) % ROWS == iota((TILE, LANES), 0) % ROWS, logs, 0.0
        )
        mass_back[unit, pl.ds(start, devices)] = jnp.sum(
            logs.reshape(devices, ROWS, LANES), axis=1, keepdims=True
        )

    spread = (iota((LANES, width), 0) // ROWS == iota((LANES, width), 1) // HD).astype(f32).astype(bf16)
    own_lane = iota((m, ROWS, LANES), 2) % ROWS == iota((m, ROWS, LANES), 1)
    ones = jnp.ones((slots, LANES), bf16)

    def combine(out_a, log_a, out_b, log_b):
        top = jnp.maximum(log_a, log_b)
        share_a, share_b = jnp.exp2(log_a - top), jnp.exp2(log_b - top)
        total = share_a + share_b
        return (share_a * out_a + share_b * out_b) / total, top + jnp.log2(total)

    def half_answers(group, phase):
        unit = 2 * phase + group
        all_copies(unit, *answers_out).wait_recv()
        all_copies(unit, *masses_out).wait_recv()
        answer[unit, me] = back[unit, me]
        mass_answer[unit, me] = mass_back[unit, me]
        outs = answer[unit].reshape(slots, width)
        rest = jnp.where(own_lane, mass_answer[unit], 0.0).reshape(slots, LANES)
        columns = [outs, ones]
        for _ in range(3):
            part = rest.astype(bf16)
            columns.append(part)
            rest = rest - part.astype(f32)
        results = []
        for local in range(per_phase):
            pos = pos_ref[group, phase * per_phase + local]
            places = iota((slots, nq), 0)
            match = jnp.concatenate(
                [(places == pos[0:1, :]).astype(f32), (places == pos[1:2, :]).astype(f32)], axis=1
            ).astype(bf16)
            picked = [
                lax.dot_general(match, c, (((0,), (0,)), ((), ())), preferred_element_type=f32)
                for c in columns
            ]
            logs = sum(
                jnp.dot(part.astype(bf16), spread, preferred_element_type=f32)
                for part in picked[2:]
            )
            there = jnp.concatenate([picked[1]] * (width // LANES), axis=1)
            logs = jnp.where(there > 0.5, logs, -1e30)
            results.append(combine(picked[0][:nq], logs[:nq], picked[0][nq:], logs[nq:]))
        return results

    def answer_mirror(phase):
        for local, (out, log) in enumerate(half_answers(1, phase)):
            step = phase * per_phase + local
            turned = log.T
            half_out[step] = out.astype(bf16)
            half_mass[step] = jnp.concatenate(
                [turned[head * HD:head * HD + 1] for head in range(heads)], axis=0
            )
        mirrored(phase, *far_answers).start()
        mirrored(phase, *far_masses).start()

    def forward(phase):
        mirrored(phase, *far_queries).wait_recv()
        send_queries(1, phase)

    far_probes.wait_recv()
    forward(0)

    @pl.loop(0, 2 * phases)
    def _(turn):
        phase = turn // 2
        odd = turn % 2
        group = jnp.where(phase == 0, odd, 1 - odd)
        unit = 2 * phase + group

        @pl.when((odd == 0) & (phase + 1 < phases))
        def _():
            forward(phase + 1)

        all_copies(unit, *queries_out).wait_recv()
        recv[unit, me] = send[unit, me]

        @pl.loop(0, slots // TILE)
        def _(tile):
            attend(unit, tile)

        @pl.loop(1, m)
        def _(index):
            copy_to(index, unit, *answers_out).start()
            copy_to(index, unit, *masses_out).start()

        @pl.when((odd == 0) & (phase > 0))
        def _():
            answer_mirror(phase - 1)

    answer_mirror(phases - 1)

    @pl.loop(0, phases)
    def _(phase):
        near = half_answers(0, phase)
        mirrored(phase, *far_answers).wait_recv()
        mirrored(phase, *far_masses).wait_recv()
        for local, (out, log) in enumerate(near):
            step = phase * per_phase + local
            other = far_mass[step]
            other = jnp.concatenate(
                [jnp.broadcast_to(other[head:head + 1], (HD, nq)) for head in range(heads)], axis=0
            ).T
            out_ref[step] = combine(out, log, far_out[step].astype(f32), other)[0].astype(bf16)

    far_probes.wait_send()

    @pl.loop(0, phases)
    def _(phase):
        mirrored(phase, *far_queries).wait_send()
        mirrored(phase, *far_answers).wait_send()
        mirrored(phase, *far_masses).wait_send()

    @pl.loop(0, 2 * phases)
    def _(unit):
        all_copies(unit, *queries_out).wait_send()
        all_copies(unit, *answers_out).wait_send()
        all_copies(unit, *masses_out).wait_send()


def body(ncol, n, queries, probes, keys, values, bucket_home, bucket_rows):
    steps, nq, width = queries.shape
    cap = max(1, 4 * nq // n)
    per_phase = min(steps, max(1, ROWS // cap))
    phases = steps // per_phase
    key_rows = keys.shape[1]
    heads = width // HD
    dims = (n, ncol, steps, nq, width, cap, per_phase, phases)
    vmem = pl.BlockSpec(memory_space=pltpu.VMEM)
    block = pltpu.VMEM((2 * phases, n // 2, ROWS, width), bf16)
    mass = pltpu.VMEM((2 * phases, n // 2, 1, LANES), f32)
    whole = pltpu.VMEM((steps, nq, width), bf16)
    whole_mass = pltpu.VMEM((steps, heads, nq), f32)
    dma = pltpu.SemaphoreType.DMA
    slots = phases * n * ROWS
    return pl.pallas_call(
        functools.partial(kernel, dims),
        out_shape=jax.ShapeDtypeStruct((steps, nq, width), bf16),
        in_specs=[vmem] * 6,
        out_specs=vmem,
        scratch_shapes=[
            pltpu.VMEM((heads, key_rows, width), bf16),
            pltpu.VMEM((heads, HD + ROWS, key_rows), bf16),
            pltpu.VMEM((2, steps, 2, nq), jnp.int32),
            whole,
            pltpu.VMEM((steps, 2, nq), jnp.int32),
            block, block, block, block, mass, mass, whole, whole, whole_mass, whole_mass,
        ] + [dma((2 * phases,))] * 6 + [dma((phases,))] * 6 + [dma((1,))] * 2,
        compiler_params=pltpu.CompilerParams(
            collective_id=0, has_side_effects=True, vmem_limit_bytes=56 * 1024 * 1024
        ),
        cost_estimate=pl.CostEstimate(
            flops=4 * slots * key_rows * width * heads,
            bytes_accessed=4 * key_rows * width,
            transcendentals=slots * key_rows * heads,
        ),
    )(
        queries,
        jnp.transpose(probes, (0, 2, 1)),
        bucket_home.reshape(1, n),
        bucket_rows.reshape(1, n),
        keys[0],
        values[0],
    )


def solution(mesh):
    ncol = mesh.shape["col"]
    n = mesh.shape["row"] * ncol
    return jax.shard_map(
        functools.partial(body, ncol, n),
        mesh=mesh,
        in_specs=(
            P(None, ("row", "col"), None),
            P(None, ("row", "col"), None),
            P(("row", "col"), None, None),
            P(("row", "col"), None, None),
            P(),
            P(),
        ),
        out_specs=P(None, ("row", "col"), None),
        check_vma=False,
    )
```

```python
import functools
import math

import jax
import jax.numpy as jnp
from jax import lax
from jax.experimental import pallas as pl
from jax.experimental.pallas import tpu as pltpu
from jax.sharding import PartitionSpec as P

HD = 32
LANES = 128
ROWS = 16
TILE = 256
SHIFT = 1.5
MESH = pl.DeviceIdType.MESH
bf16 = jnp.bfloat16
f32 = jnp.float32


def iota(shape, dim):
    return lax.broadcasted_iota(jnp.int32, shape, dim)


def kernel(
    dims, q_ref, probe_ref, home_ref, rows_ref, k_ref, v_ref, out_ref,
    keys_by_head, values_by_head, pos_ref, send, recv, back, answer, send_sem, recv_sem, back_sem, answer_sem,
):
    n, ncol, steps, nq, width, cap, per_phase, phases = dims
    heads = width // HD
    key_rows = k_ref.shape[0]
    slots = n * ROWS
    scale = math.log2(math.e) / math.sqrt(HD)
    me = lax.axis_index("row") * ncol + lax.axis_index("col")

    def peer(index):
        other = lax.rem(me + index, n)
        return other, (other // ncol, lax.rem(other, ncol))

    barrier = pltpu.get_barrier_semaphore()

    @pl.loop(1, n)
    def _(index):
        _, where = peer(index)
        pl.semaphore_signal(barrier, inc=1, device_id=where, device_id_type=MESH)

    def copy_to(index, phase, source, target, source_sem, target_sem):
        other, where = peer(index)
        return pltpu.make_async_remote_copy(
            src_ref=source.at[phase, other],
            dst_ref=target.at[phase, me],
            send_sem=source_sem.at[phase],
            recv_sem=target_sem.at[phase],
            device_id=where,
            device_id_type=MESH,
        )

    def all_copies(phase, source, target, source_sem, target_sem):
        _, where = peer(1)
        return pltpu.make_async_remote_copy(
            src_ref=source.at[phase, pl.ds(0, n - 1)],
            dst_ref=target.at[phase, pl.ds(0, n - 1)],
            send_sem=source_sem.at[phase],
            recv_sem=target_sem.at[phase],
            device_id=where,
            device_id_type=MESH,
        )

    queries_out = (send, recv, send_sem, recv_sem)
    answers_out = (back, answer, back_sem, answer_sem)

    home_row = home_ref[...]
    diagonal = iota((n, n), 0) == iota((n, n), 1)
    home_column = jnp.sum(jnp.where(diagonal, home_row, 0), axis=1, keepdims=True).astype(f32)
    before = (iota((nq, nq), 0) < iota((nq, nq), 1)).astype(bf16)

    def slot_rows(step):
        ids = probe_ref[step]
        first = (iota((n, nq), 0) == ids[0:1, :]).astype(f32)
        second = (iota((n, nq), 0) == ids[1:2, :]).astype(f32)
        both = jnp.concatenate([first, second], axis=0).astype(bf16)
        earlier = jnp.dot(both, before, preferred_element_type=f32)
        offset = jnp.sum(first, axis=1, keepdims=True)
        order_first = jnp.sum(first * (earlier[:n] + home_column * ROWS), axis=0, keepdims=True)
        order_second = jnp.sum(
            second * (earlier[n:] + offset + home_column * ROWS), axis=0, keepdims=True
        )
        shift = (step % per_phase) * cap
        return jnp.concatenate([order_first, order_second], axis=0).astype(jnp.int32) + shift

    def arrange(phase):
        total = None
        for local in range(per_phase):
            step = phase * per_phase + local
            pos = slot_rows(step)
            pos_ref[step] = pos
            places = iota((slots, nq), 0)
            match = ((places == pos[0:1, :]) | (places == pos[1:2, :])).astype(f32).astype(bf16)
            part = jnp.dot(match, q_ref[step], preferred_element_type=f32)
            total = part if total is None else total + part
        send[phase] = total.astype(bf16).reshape(n, ROWS, width)

    def send_queries(phase):
        @pl.loop(1, n)
        def _(index):
            copy_to(index, phase, *queries_out).start()

    arrange(0)
    pl.semaphore_wait(barrier, n - 1)
    send_queries(0)

    @pl.loop(1, phases)
    def _(phase):
        arrange(phase)
        send_queries(phase)

    mine = jnp.sum(jnp.where(home_row == me, rows_ref[...], 0), axis=1, keepdims=True)
    valid = iota((key_rows, width), 0) < mine
    keys_all = k_ref[...].astype(f32)
    keys_all = jnp.where(valid, keys_all, keys_all[0:1, :])
    values_all = jnp.where(valid, v_ref[...].astype(f32), 0.0).T
    counted = (iota((ROWS, key_rows), 1) < mine).astype(f32)
    for head in range(heads):
        keys_by_head[head] = jnp.where(
            iota((key_rows, width), 1) // HD == head, keys_all, 0.0
        ).astype(bf16)
        values_by_head[head] = jnp.concatenate(
            [values_all[head * HD:(head + 1) * HD], counted], axis=0
        ).astype(bf16)

    def attend(phase, tile):
        devices = TILE // ROWS
        start = pl.multiple_of(tile * devices, devices)
        queries = recv[phase, pl.ds(start, devices)].reshape(TILE, width)
        queries = queries.astype(f32).T.astype(bf16)
        pieces, logs = [], []
        following = jnp.dot(keys_by_head[0], queries, preferred_element_type=f32)
        for head in range(heads):
            scores = following
            if head + 1 < heads:
                following = jnp.dot(keys_by_head[head + 1], queries, preferred_element_type=f32)
            top = jnp.max(scores.reshape(-1, LANES, TILE), axis=0)
            top = jnp.max(top, axis=0, keepdims=True) * scale - SHIFT
            weights = jnp.exp2((scores * scale - top).astype(bf16))
            mixed = jnp.dot(values_by_head[head], weights, preferred_element_type=f32)
            total = mixed[HD:HD + 1]
            pieces.append(mixed[:HD] * (1.0 / total))
            logs.append(top + jnp.log2(total))
        rest = jnp.concatenate(logs, axis=0)
        for _ in range(3):
            part = rest.astype(bf16).astype(f32)
            pieces.append(part)
            rest = rest - part
        pieces.append(jnp.zeros((LANES - 3 * heads, TILE), f32))
        back[phase, pl.ds(start, devices)] = (
            jnp.concatenate(pieces, axis=0).T.astype(bf16).reshape(devices, ROWS, width + LANES)
        )

    @pl.loop(0, phases)
    def _(phase):
        all_copies(phase, *queries_out).wait_recv()
        recv[phase, me] = send[phase, me]

        @pl.loop(0, slots // TILE)
        def _(tile):
            attend(phase, tile)

        @pl.loop(1, n)
        def _(index):
            copy_to(index, phase, *answers_out).start()

    source = iota((LANES, width), 0)
    spread = (source % heads == iota((LANES, width), 1) // HD) & (source < 3 * heads)
    spread = spread.astype(f32).astype(bf16)

    @pl.loop(0, phases)
    def _(phase):
        all_copies(phase, *answers_out).wait_recv()
        answer[phase, me] = back[phase, me]
        outs = answer[phase].reshape(slots, width + LANES)
        for local in range(per_phase):
            step = phase * per_phase + local
            pos = pos_ref[step]
            places = iota((slots, nq), 0)
            match = jnp.concatenate(
                [(places == pos[0:1, :]).astype(f32), (places == pos[1:2, :]).astype(f32)], axis=1
            ).astype(bf16)
            picked = lax.dot_general(
                match, outs, (((0,), (0,)), ((), ())), preferred_element_type=f32
            )
            logs = jnp.dot(picked[:, width:].astype(bf16), spread, preferred_element_type=f32)
            picked = picked[:, :width]
            share = 1.0 / (1.0 + jnp.exp2(logs[nq:] - logs[:nq]))
            merged = picked[nq:] + share * (picked[:nq] - picked[nq:])
            out_ref[step] = merged.astype(bf16)

    @pl.loop(0, phases)
    def _(phase):
        all_copies(phase, *queries_out).wait_send()
        all_copies(phase, *answers_out).wait_send()


def body(ncol, n, queries, probes, keys, values, bucket_home, bucket_rows):
    steps, nq, width = queries.shape
    cap = max(1, 4 * nq // n)
    per_phase = min(steps, max(1, ROWS // cap))
    phases = steps // per_phase
    key_rows = keys.shape[1]
    heads = width // HD
    dims = (n, ncol, steps, nq, width, cap, per_phase, phases)
    vmem = pl.BlockSpec(memory_space=pltpu.VMEM)
    block = pltpu.VMEM((phases, n, ROWS, width), bf16)
    wide = pltpu.VMEM((phases, n, ROWS, width + LANES), bf16)
    slots = phases * n * ROWS
    return pl.pallas_call(
        functools.partial(kernel, dims),
        out_shape=jax.ShapeDtypeStruct((steps, nq, width), bf16),
        in_specs=[vmem] * 6,
        out_specs=vmem,
        scratch_shapes=[
            pltpu.VMEM((heads, key_rows, width), bf16),
            pltpu.VMEM((heads, HD + ROWS, key_rows), bf16),
            pltpu.VMEM((steps, 2, nq), jnp.int32),
            block, block, wide, wide,
        ] + [pltpu.SemaphoreType.DMA((phases,))] * 4,
        compiler_params=pltpu.CompilerParams(
            collective_id=0, has_side_effects=True, vmem_limit_bytes=56 * 1024 * 1024
        ),
        cost_estimate=pl.CostEstimate(
            flops=4 * slots * key_rows * width * heads,
            bytes_accessed=4 * key_rows * width,
            transcendentals=slots * key_rows * heads,
        ),
    )(
        queries,
        jnp.transpose(probes, (0, 2, 1)),
        bucket_home.reshape(1, n),
        bucket_rows.reshape(1, n),
        keys[0],
        values[0],
    )


def solution(mesh):
    ncol = mesh.shape["col"]
    n = mesh.shape["row"] * ncol
    return jax.shard_map(
        functools.partial(body, ncol, n),
        mesh=mesh,
        in_specs=(
            P(None, ("row", "col"), None),
            P(None, ("row", "col"), None),
            P(("row", "col"), None, None),
            P(("row", "col"), None, None),
            P(),
            P(),
        ),
        out_specs=P(None, ("row", "col"), None),
        check_vma=False,
    )
```
